32 devices in a mesh: groups: 2 (over y), tp: 8 (over z, x), sq: 2 (over core).
Axes of the slice: x: 2, y: 2, z: 4, core: 2. Of those that a mesh axis runs over, the one named last changes fastest.
Arguments:
- hidden_states: bfloat16 [1024, 8192], P(('groups', 'sq'), 'tp'), parts along dimension 0, may hold values from -41 to 41
- out_grad: bfloat16 [1024, 8192], P(('groups', 'sq'), 'tp'), parts along dimension 0, may hold values from -6 to 6
- norm_gain: bfloat16 [8192], P('tp'), may hold values from 0.099609375 to 1.8984375
- w_gate: bfloat16 [8192, 16384], P('sq', 'tp'), may hold values from -0.0625 to 0.0625
- w_up: bfloat16 [8192, 16384], P('sq', 'tp'), may hold values from -0.0625 to 0.0625
- w_down: bfloat16 [16384, 8192], P('tp', 'sq'), may hold values from -0.046875 to 0.046875
- proj_model: bfloat16 [3, 8192, 64], P(None, 'tp'), may hold values from -0.0625 to 0.0625
- proj_hidden: bfloat16 [3, 16384, 64], P(None, 'tp'), may hold values from -0.046875 to 0.046875
- queries: bfloat16 [3, 256, 4096], P(None, ('tp', 'sq')), may hold values from -0.009765625 to 0.009765625
Outputs:
- scores: float32 [4, 256], P(('groups', 'sq'), 'tp'), parts along dimension 0
The draws below stay inside these ranges and needn't reach their ends.
There are 2 independent parts, one for each index of `groups`. The reference program is written for one: setup_inputs(seed, part) draws one part's arguments, and reference() takes and returns one part's arrays. A program takes and returns all parts, laid end to end along the dimension named above; an argument that names none is the same for every part. Nothing has to cross between parts.
All inputs are finite; a program needn't handle non-finite values.
Results may differ from the reference program's by a relative error of at most 0.0052.
Values may be sent and summed in bfloat16 or wider, within the bound.
A program may use at most 320 MiB of HBM per device.

```python
import jax
import jax.numpy as jnp
from jax import lax

D = 8192
HID = 16384
R = 64
SEQ_LEN = 256
EXAMPLES = 2
TOKENS = 512
NQ = 256


def draw_hidden_states(key, part):
    key = jax.random.fold_in(key, 11)
    first_key = jax.random.fold_in(key, 0)
    shape = (TOKENS, D)
    column_pos = jnp.arange(D, dtype=jnp.float32) / D
    column_scale = 1.0 + 0.75 * column_pos
    values = jnp.clip(jax.random.normal(first_key, shape, jnp.float32), -6.0, 6.0) * column_scale
    return values.astype(jnp.bfloat16)


def steps_of(stream_key, dims, cuts, low, high):
    factor_of, own = 1.0, jax.random.fold_in(stream_key, 6)
    for axis_at, shards_of in cuts:
        steps = jnp.exp(jax.random.uniform(jax.random.fold_in(own, axis_at), (shards_of,), jnp.float32, low / len(cuts), high / len(cuts)))
        factor_of = factor_of * jnp.repeat(steps, dims[axis_at] // shards_of).reshape([-1 if axis == axis_at else 1 for axis in range(len(dims))])
    return factor_of


def scatter_about(own_key, dims, spread, most, pieces=(), held_as=jnp.bfloat16):
    values = spread * jax.random.normal(own_key, dims, jnp.float32)
    if pieces:
        values = values * steps_of(own_key, dims, pieces, -0.22, 0.18)
    return jnp.clip(values, -most, most).astype(held_as)


def setup_inputs(seed: int = 0, part: int = 0) -> dict:
    seeds = jax.random.split(jax.random.key(seed), 10)
    own_keys = jax.random.split(jax.random.fold_in(seeds[9], part), 10)
    hidden_states = draw_hidden_states(jax.random.fold_in(jax.random.fold_in(seeds[9], part), 71), part)
    out_grad = scatter_about(own_keys[1], (TOKENS, D), 1.0, 6.0, ((0, 2), (1, 8)))
    norm_gain = jnp.clip(1.0 + 0.18 * jax.random.normal(seeds[2], (D,), jnp.float32), 0.099609375, 1.8984375).astype(jnp.bfloat16)
    w_gate = scatter_about(seeds[3], (D, HID), D ** -0.5, 0.0625, ((0, 2), (1, 8)))
    w_up = scatter_about(seeds[4], (D, HID), D ** -0.5, 0.0625, ((0, 2), (1, 8)))
    w_down = scatter_about(seeds[5], (HID, D), HID ** -0.5, 0.046875, ((0, 8), (1, 2)))
    proj_model = scatter_about(seeds[6], (3, D, R), D ** -0.5, 0.0625, ((1, 8),))
    proj_hidden = scatter_about(seeds[7], (3, HID, R), HID ** -0.5, 0.046875, ((1, 8),))
    queries = scatter_about(seeds[8], (3, NQ, R * R), (3 * R * R * SEQ_LEN // 8) ** -0.5, 0.009765625, ((1, 16),))
    return {"hidden_states": hidden_states, "out_grad": out_grad, "norm_gain": norm_gain, "w_gate": w_gate, "w_up": w_up, "w_down": w_down, "proj_model": proj_model, "proj_hidden": proj_hidden, "queries": queries}


EPS = 1e-05

def layer_features(columns, member):
    slot_pairs = ((3, 0), (4, 1), (2, 5))
    result = []
    for out_slot, in_slot in slot_pairs:
        outer = columns[:, out_slot * R:(out_slot + 1) * R]
        inner = columns[:, in_slot * R:(in_slot + 1) * R]
        block = jnp.einsum('te,to,ti->eoi', member, outer, inner, precision=lax.Precision.HIGHEST)
        result.append(block.reshape(member.shape[1], R * R))
    return jnp.stack(result, axis=1)

def reference(hidden_states, out_grad, norm_gain, w_gate, w_up, w_down, proj_model, proj_hidden, queries):
    states = hidden_states.astype(jnp.float32)
    row_sq = lax.optimization_barrier(jnp.mean(states * states, axis=1, keepdims=True))
    normed = (states * lax.rsqrt(row_sq + EPS) * norm_gain.astype(jnp.float32)).astype(jnp.bfloat16)
    gate = jnp.dot(normed, w_gate, preferred_element_type=jnp.float32)
    upward = jnp.dot(normed, w_up, preferred_element_type=jnp.float32)
    sigmoid_gate = jax.nn.sigmoid(gate)
    swish = gate * sigmoid_gate
    activation = (swish * upward).astype(jnp.bfloat16)
    grad_act = jnp.dot(out_grad, w_down.T, preferred_element_type=jnp.float32)
    grad_gate = (grad_act * upward * sigmoid_gate * (1.0 + gate * (1.0 - sigmoid_gate))).astype(jnp.bfloat16)
    grad_up = (grad_act * swish).astype(jnp.bfloat16)
    sources = (normed, normed, out_grad, grad_gate, grad_up, activation)
    tables = (proj_model[0], proj_model[1], proj_model[2], proj_hidden[0], proj_hidden[1], proj_hidden[2])
    columns = jnp.concatenate([jnp.dot(source, table, preferred_element_type=jnp.float32) for source, table in zip(sources, tables)], axis=1)
    token_seq = jnp.arange(TOKENS, dtype=jnp.int32) // SEQ_LEN
    member = (token_seq[:, None] == jnp.arange(EXAMPLES, dtype=jnp.int32)[None, :]).astype(jnp.float32)
    features = layer_features(columns, member)
    return jnp.einsum('elk,lqk->eq', features, queries.astype(jnp.float32), precision=lax.Precision.HIGHEST)
```

```python
import functools

import jax
import jax.numpy as jnp
from jax import lax
from jax.experimental import pallas as pl
from jax.experimental.pallas import tpu as pltpu
from jax.sharding import PartitionSpec as P

D = 8192
R = 64
SEQ_LEN = 256
EPS = 1e-05
NB = 2
NC = 4
MESH = pl.DeviceIdType.MESH
HIGH = lax.Precision.HIGHEST
ARRIVALS = (
    (0, 2, 4, 6),
    (0, 1, 2, 4),
    (0, 1, 2, 3),
    (0, 1, 3, 5),
    (1, 3, 5, 7),
    (3, 5, 6, 7),
    (4, 5, 6, 7),
    (2, 4, 6, 7),
)


def dot(a, b, dims=((1,), (0,)), precision=None):
    return lax.dot_general(a, b, (dims, ((), ())), precision=precision, preferred_element_type=jnp.float32)


def kernel(
    hid_ref, og_ref, gain_ref, wg_ref, wu_ref, wd_ref, pm_ref, ph_ref, q_ref, out_ref,
    hid, og, nm, pm, ph, qb, rs, grid_in, wdb, wgb, wub, acc_a, acc_gu, rec_a, rec_gu, cols, cols_in, feat, feat_in,
    load_sem, w_sem, g_recv, own_send, core_send, relay_send, rs_send, rs_recv, q_send, q_recv,
    pa_send, pa_recv, px_send, px_recv, c_send, c_recv, f_send, f_recv,
):
    t = lax.axis_index("tp")
    s = lax.axis_index("sq")
    o = 1 - s
    rows, width = hid.shape
    bt = rows // NB
    hl = acc_a.shape[1]
    nc = hl // NC
    share = bt // 8

    def t_of(p):
        return jnp.where(p < 4, 2 * p, 15 - 2 * p)

    zz = t // 2
    pos = jnp.where(t % 2 == 0, zz, 7 - zz)
    right = t_of((pos + 1) % 8)
    left = t_of((pos + 7) % 8)
    place = (pos + 2 + 4 * s) % 8
    half = t // 4
    slot = t % 4

    def remote(src, dst, send, recv, dev):
        return pltpu.make_async_remote_copy(
            src_ref=src, dst_ref=dst, send_sem=send, recv_sem=recv, device_id=dev, device_id_type=MESH
        )

    loads = [
        pltpu.make_async_copy(hid_ref, hid, load_sem.at[0]),
        pltpu.make_async_copy(og_ref, og, load_sem.at[1]),
        pltpu.make_async_copy(pm_ref, pm, load_sem.at[2]),
        pltpu.make_async_copy(ph_ref, ph, load_sem.at[3]),
        pltpu.make_async_copy(q_ref, qb.at[s], load_sem.at[4]),
    ]
    for c in loads:
        c.start()

    steps = []
    for i in range(4):
        j = jnp.int32(0)
        for c in range(8):
            j = j + jnp.where(place == c, ARRIVALS[c][i], 0)
        dist = (j + 1) // 2
        odd = j % 2
        src_pos = (pos + 8 + dist * (1 - 2 * odd)) % 8
        src_slot = t_of(src_pos) % 4
        target = jnp.where(odd == 1, right, left)
        passes = [
            (j >= 1) & (dist < jnp.where(odd == 1, 4, 3)),
            (j >= 1) & (dist < jnp.where(odd == 1, 3, 4)),
        ]
        steps.append((src_slot, target, passes))

    def w_load(a, i):
        at = steps[i][0] * width
        at = pl.multiple_of(at, width)
        if a == 0:
            return [pltpu.make_async_copy(wd_ref.at[:, pl.ds(at, width)], wdb.at[i % 2], w_sem.at[0, i % 2])]
        return [
            pltpu.make_async_copy(wg_ref.at[pl.ds(at, width), :], wgb.at[i % 2], w_sem.at[1, i % 2]),
            pltpu.make_async_copy(wu_ref.at[pl.ds(at, width), :], wub.at[i % 2], w_sem.at[2, i % 2]),
        ]

    for a in range(2):
        for i in range(2):
            for c in w_load(a, i):
                c.start()

    barrier = pltpu.get_barrier_semaphore()
    for d in range(1, 8):
        pl.semaphore_signal(barrier, inc=1, device_id={"tp": (t + d) % 8}, device_id_type=MESH)
    for tt in (t, left, right):
        pl.semaphore_signal(barrier, inc=1, device_id={"tp": tt, "sq": o}, device_id_type=MESH)
    pl.semaphore_wait(barrier, 10)

    def own_copies(a, b):
        at = pl.ds(pl.multiple_of(b * bt, bt), bt)
        src = og_ref.at[at, :] if a == 0 else nm.at[at, :]
        dst = grid_in.at[a, b, slot, s]
        recv = g_recv.at[a, b, slot, s]
        away = [
            remote(src, dst, own_send.at[a, b, 0], recv, {"tp": right, "sq": half}),
            remote(src, dst, own_send.at[a, b, 1], recv, {"tp": left, "sq": half}),
        ]
        core = remote(src, dst, core_send.at[a, b], recv, {"sq": o})
        here = pltpu.make_async_copy(src, dst, recv)
        return away, core, here

    def own_start(a, b):
        away, core, here = own_copies(a, b)
        for c in away:
            c.start()

        @pl.when(half != s)
        def _():
            core.start()

        @pl.when(half == s)
        def _():
            here.start()

    own_start(0, 0)
    q_copy = remote(q_ref, qb.at[s], q_send, q_recv, {"sq": o})
    q_copy.start()

    loads[0].wait()
    states = hid[...].astype(jnp.float32)
    sums = jnp.sum(states * states, axis=1, keepdims=True)
    rs[0] = jnp.transpose(jnp.broadcast_to(sums, (rows, 128)))[0:8]
    rs_copies = [
        remote(rs.at[0], rs.at[d], rs_send.at[d], rs_recv.at[d], {"tp": (t + d) % 8}) for d in range(1, 8)
    ]
    for c in rs_copies:
        c.start()
    loads[1].wait()
    loads[2].wait()
    c2 = dot(og[...], pm[2])
    for c in rs_copies:
        c.wait_recv()
    total = rs[0]
    for d in range(1, 8):
        total = total + rs[d]
    factor = lax.rsqrt(total / D + EPS)
    factor = jnp.transpose(jnp.broadcast_to(factor[0:1], (128, rows)))[:, 0:1]
    nm[...] = (hid[...].astype(jnp.float32) * factor * gain_ref[...].astype(jnp.float32)).astype(jnp.bfloat16)
    own_start(1, 0)
    c0 = dot(nm[...], pm[0])
    c1 = dot(nm[...], pm[1])
    for b in range(NB):
        part = slice(b * bt, (b + 1) * bt)
        cols[b, :, 0:128] = jnp.concatenate([c0[part], c1[part]], axis=1)
        cols[b, :, 128:256] = jnp.concatenate([c2[part], c2[part]], axis=1)
    loads[3].wait()

    def relays(a, b, i, k):
        src_slot, target, passes = steps[i]
        chunk = grid_in.at[a, b, src_slot, k]
        copy = remote(
            chunk, chunk, relay_send.at[a, b, i, k], g_recv.at[a, b, src_slot, k], {"tp": target}
        )
        return copy, passes[k]

    def arrive(a, b, i):
        for k in range(2):
            copy, passing = relays(a, b, i, k)
            copy.wait_recv()

            @pl.when(passing)
            def _():
                copy.start()

    def refill(a, b, i):
        if i < 2:
            for c in w_load(a, i + 2):
                c.start()
        else:

            @pl.when(b + 1 < NB)
            def _():
                for c in w_load(a, i - 2):
                    c.start()

    def pa_copy(b):
        return remote(
            acc_a.at[pl.ds(pl.multiple_of(o * bt, bt), bt), :], rec_a.at[b], pa_send.at[b], pa_recv.at[b], {"sq": o}
        )

    def px_copy(b, n):
        lanes = pl.ds(pl.multiple_of(n * nc, nc), nc)
        return remote(
            acc_gu.at[:, pl.ds(pl.multiple_of(o * bt, bt), bt), lanes],
            rec_gu.at[b, :, :, lanes],
            px_send.at[b, n],
            px_recv.at[b, n],
            {"sq": o},
        )

    def c_copy(b, d):
        peer = (t + d) % 8
        return remote(
            cols.at[b, pl.ds(pl.multiple_of(peer * share, share), share), :],
            cols_in.at[b, d],
            c_send.at[b, d],
            c_recv.at[b, d],
            {"tp": peer},
        )

    def block(b, carry):
        @pl.when(b + 1 < NB)
        def _():
            own_start(0, b + 1)

        for i in range(4):
            arrive(0, b, i)
            for c in w_load(0, i):
                c.wait()
            src_slot = steps[i][0]

            def down(n, carry):
                lanes = pl.ds(pl.multiple_of(n * nc, nc), nc)
                lhs = grid_in[0, b, src_slot].reshape(2 * bt, width)
                got = dot(lhs, wdb[i % 2, lanes, :], ((1,), (1,)))
                acc_a[:, lanes] = got if i == 0 else acc_a[:, lanes] + got
                return carry

            lax.fori_loop(0, NC, down, 0)
            refill(0, b, i)
        pa_copy(b).start()

        @pl.when(b + 1 < NB)
        def _():
            own_start(1, b + 1)

        for i in range(4):
            arrive(1, b, i)
            for c in w_load(1, i):
                c.wait()
            src_slot = steps[i][0]

            def gate_up(n, carry):
                lanes = pl.ds(pl.multiple_of(n * nc, nc), nc)
                lhs = grid_in[1, b, src_slot].reshape(2 * bt, width)
                for m, buf in ((0, wgb), (1, wub)):
                    got = dot(lhs, buf[i % 2, :, lanes])
                    acc_gu[m, :, lanes] = got if i == 0 else acc_gu[m, :, lanes] + got
                if i == 3:
                    px_copy(b, n).start()
                return carry

            lax.fori_loop(0, NC, gate_up, 0)
            refill(1, b, i)

        pa_copy(b).wait_recv()
        mine = pl.ds(pl.multiple_of(s * bt, bt), bt)

        def hidden(n, carry):
            px_copy(b, n).wait_recv()
            lanes = pl.ds(pl.multiple_of(n * nc, nc), nc)
            gate = acc_gu[0, mine, lanes] + rec_gu[b, 0, :, lanes]
            upward = acc_gu[1, mine, lanes] + rec_gu[b, 1, :, lanes]
            grad_act = acc_a[mine, lanes] + rec_a[b, :, lanes]
            sig = jax.nn.sigmoid(gate)
            swish = gate * sig
            activation = (swish * upward).astype(jnp.bfloat16)
            grad_gate = (grad_act * upward * sig * (1.0 + gate * (1.0 - sig))).astype(jnp.bfloat16)
            grad_up = (grad_act * swish).astype(jnp.bfloat16)
            return (
                carry[0] + dot(grad_gate, ph[0, lanes, :]),
                carry[1] + dot(grad_up, ph[1, lanes, :]),
                carry[2] + dot(activation, ph[2, lanes, :]),
            )

        zero = jnp.zeros((bt, R), jnp.float32)
        c3, c4, c5 = lax.fori_loop(0, NC, hidden, (zero, zero, zero))
        cols[b, :, 128:256] = jnp.concatenate([cols[b, :, 128:192], c3], axis=1)
        cols[b, :, 256:384] = jnp.concatenate([c4, c5], axis=1)
        for d in range(1, 8):
            c_copy(b, d).start()
        pa_copy(b).wait_send()
        for n in range(NC):
            px_copy(b, n).wait_send()
        return carry

    lax.fori_loop(0, NB, block, 0)

    tokens = []
    for b in range(NB):
        whole = cols[b, pl.ds(pl.multiple_of(t * share, share), share), :]
        for d in range(1, 8):
            c_copy(b, d).wait_recv()
            whole = whole + cols_in[b, d]
        tokens.append(whole)
    tokens = jnp.concatenate(tokens, axis=0)
    row = lax.broadcasted_iota(jnp.int32, (R, R), 0)
    col = lax.broadcasted_iota(jnp.int32, (R, R), 1)
    order = jnp.where(row < R // 2, 2 * row, 2 * row - R + 1)
    pick = (col == order).astype(jnp.float32)
    for layer, (out_slot, in_slot) in enumerate(((3, 0), (4, 1), (2, 5))):
        outer = tokens[:, out_slot * R : (out_slot + 1) * R]
        inner = tokens[:, in_slot * R : (in_slot + 1) * R]
        pair = dot(outer, inner, ((0,), (0,)), HIGH)
        pair = dot(pick, pair, precision=HIGH)
        feat[layer * 32 : (layer + 1) * 32] = jnp.concatenate([pair[0:32], pair[32:64]], axis=1)
    f_copies = [remote(feat, feat_in.at[d], f_send.at[d], f_recv.at[d], {"tp": (t + d) % 8}) for d in range(1, 8)]
    for c in f_copies:
        c.start()
    loads[4].wait()
    q_copy.wait_recv()
    whole = feat[...]
    for d in range(1, 8):
        f_copies[d - 1].wait_recv()
        whole = whole + feat_in[d]
    acc = jnp.zeros((2, 16, 128), jnp.float32)
    for layer in range(3):
        for j in range(32):
            line = whole[layer * 32 + j : layer * 32 + j + 1]
            acc = acc + qb[:, layer, :, j * 128 : (j + 1) * 128].astype(jnp.float32) * line[None]
    out_ref[...] = dot(jnp.ones((1, 128), jnp.float32), acc.reshape(32, 128), ((1,), (1,)), HIGH)

    q_copy.wait_send()
    for c in rs_copies + f_copies:
        c.wait_send()

    def drain(b, carry):
        for a in range(2):
            away, core, _ = own_copies(a, b)
            for c in away:
                c.wait_send()

            @pl.when(half != s)
            def _():
                core.wait_send()

            for i in range(4):
                for k in range(2):
                    copy, passing = relays(a, b, i, k)

                    @pl.when(passing)
                    def _():
                        copy.wait_send()

        for d in range(1, 8):
            c_copy(b, d).wait_send()
        return carry

    lax.fori_loop(0, NB, drain, 0)


def ring_device(hidden_states, out_grad, norm_gain, w_gate, w_up, w_down, proj_model, proj_hidden, queries):
    rows, width = hidden_states.shape
    hl = w_gate.shape[1]
    bt = rows // NB
    share = bt // 8
    bf, f32 = jnp.bfloat16, jnp.float32
    dma = pltpu.SemaphoreType.DMA
    anywhere = pl.BlockSpec(memory_space=pl.ANY)
    vmem = pl.BlockSpec(memory_space=pltpu.VMEM)
    return pl.pallas_call(
        kernel,
        out_shape=jax.ShapeDtypeStruct((1, 32), f32),
        in_specs=[anywhere, anywhere, vmem] + [anywhere] * 6,
        out_specs=vmem,
        scratch_shapes=[
            pltpu.VMEM((rows, width), bf),
            pltpu.VMEM((rows, width), bf),
            pltpu.VMEM((rows, width), bf),
            pltpu.VMEM(proj_model.shape, bf),
            pltpu.VMEM(proj_hidden.shape, bf),
            pltpu.VMEM((2,) + queries.shape, bf),
            pltpu.VMEM((8, 8, rows), f32),
            pltpu.VMEM((2, NB, 4, 2, bt, width), bf),
            pltpu.VMEM((2, hl, width), bf),
            pltpu.VMEM((2, width, hl), bf),
            pltpu.VMEM((2, width, hl), bf),
            pltpu.VMEM((2 * bt, hl), f32),
            pltpu.VMEM((2, 2 * bt, hl), f32),
            pltpu.VMEM((NB, bt, hl), f32),
            pltpu.VMEM((NB, 2, bt, hl), f32),
            pltpu.VMEM((NB, bt, 6 * R), f32),
            pltpu.VMEM((NB, 8, share, 6 * R), f32),
            pltpu.VMEM((96, 128), f32),
            pltpu.VMEM((8, 96, 128), f32),
            dma((5,)),
            dma((3, 2)),
            dma((2, NB, 4, 2)),
            dma((2, NB, 2)),
            dma((2, NB)),
            dma((2, NB, 4, 2)),
            dma((8,)),
            dma((8,)),
            dma,
            dma,
            dma((NB,)),
            dma((NB,)),
            dma((NB, NC)),
            dma((NB, NC)),
            dma((NB, 8)),
            dma((NB, 8)),
            dma((8,)),
            dma((8,)),
        ],
        compiler_params=pltpu.CompilerParams(
            collective_id=0, has_side_effects=True, vmem_limit_bytes=60 * 1024 * 1024
        ),
        cost_estimate=pl.CostEstimate(flops=26 * 10**9, bytes_accessed=10**8, transcendentals=10**6),
    )(
        hidden_states, out_grad, norm_gain.reshape(1, width), w_gate, w_up, w_down, proj_model, proj_hidden, queries
    )


def layer_features(columns, member):
    slot_pairs = ((3, 0), (4, 1), (2, 5))
    result = []
    for out_slot, in_slot in slot_pairs:
        outer = columns[:, out_slot * R : (out_slot + 1) * R]
        inner = columns[:, in_slot * R : (in_slot + 1) * R]
        block = jnp.einsum("te,to,ti->eoi", member, outer, inner, precision=HIGH)
        result.append(block.reshape(member.shape[1], R * R))
    return jnp.stack(result, axis=1)


def membership(row_count, seq_count):
    token_seq = jnp.arange(row_count, dtype=jnp.int32) // SEQ_LEN
    return (token_seq[:, None] == jnp.arange(seq_count, dtype=jnp.int32)[None, :]).astype(jnp.float32)


def wide_device(hidden_states, out_grad, norm_gain, w_gate, w_up, w_down, proj_model, proj_hidden, queries):
    gate_full, up_full, down_full = (
        lax.all_gather(w_gate, "sq", axis=0, tiled=True),
        lax.all_gather(w_up, "sq", axis=0, tiled=True),
        lax.all_gather(w_down, "sq", axis=1, tiled=True),
    )
    row_count = hidden_states.shape[0]
    seq_count = row_count // SEQ_LEN
    states = hidden_states.astype(jnp.float32)
    row_total = lax.psum(jnp.sum(states * states, axis=1), "tp")
    factor = lax.rsqrt(row_total / D + EPS)
    normed = (states * factor[:, None] * norm_gain.astype(jnp.float32)).astype(jnp.bfloat16)
    shard_piece = lax.all_gather(normed, "tp", axis=1, tiled=True)
    gate = jnp.dot(shard_piece, gate_full, preferred_element_type=jnp.float32)
    upward = jnp.dot(shard_piece, up_full, preferred_element_type=jnp.float32)
    grad_act = lax.dot_general(
        lax.all_gather(out_grad, "tp", axis=1, tiled=True),
        down_full,
        (((1,), (1,)), ((), ())),
        preferred_element_type=jnp.float32,
    )
    sigmoid_gate = jax.nn.sigmoid(gate)
    swish = gate * sigmoid_gate
    activation = (swish * upward).astype(jnp.bfloat16)
    grad_gate = (grad_act * upward * sigmoid_gate * (1.0 + gate * (1.0 - sigmoid_gate))).astype(jnp.bfloat16)
    grad_up = (grad_act * swish).astype(jnp.bfloat16)
    sources = (normed, normed, out_grad, grad_gate, grad_up, activation)
    pieces = []
    for i, source in enumerate(sources):
        table = proj_model[i] if i < 3 else proj_hidden[i - 3]
        pieces.append(jnp.dot(source, table, preferred_element_type=jnp.float32))
    columns = lax.psum(jnp.concatenate(pieces, axis=1), "tp")
    features = layer_features(columns, membership(row_count, seq_count))
    paired = lax.all_gather(queries, "sq", axis=1, tiled=True)
    return jnp.einsum("elk,lqk->eq", features, paired.astype(jnp.float32), precision=HIGH)


def solution(mesh):
    placed = (
        P(("groups", "sq"), "tp"),
        P(("groups", "sq"), "tp"),
        P("tp"),
        P("sq", "tp"),
        P("sq", "tp"),
        P("tp", "sq"),
        P(None, "tp", None),
        P(None, "tp", None),
        P(None, ("tp", "sq"), None),
    )
    body = ring_device if mesh.shape["tp"] == 8 else wide_device
    return jax.shard_map(
        body, mesh=mesh, in_specs=placed, out_specs=P(("groups", "sq"), "tp"), check_vma=False
    )
```

```python
import functools

import jax
import jax.numpy as jnp
from jax import lax
from jax.experimental import pallas as pl
from jax.experimental.pallas import tpu as pltpu
from jax.sharding import PartitionSpec as P

D = 8192
R = 64
SEQ_LEN = 256
EPS = 1e-05
NB = 2
NC = 4
MESH = pl.DeviceIdType.MESH
HIGH = lax.Precision.HIGHEST
ORDER = tuple(sorted(((r, i) for r in range(2 * NB) for i in range(4)), key=lambda e: 7 * e[0] + 6 * e[1]))
EARLY = 2
FINISH_AFTER = ORDER[ORDER.index((2, 3)) + 1]
USES = tuple(tuple(e for e in ORDER if e[0] // NB == a) for a in range(2))
ARRIVALS = (
    (0, 2, 4, 6),
    (0, 1, 2, 4),
    (0, 1, 2, 3),
    (0, 1, 3, 5),
    (1, 3, 5, 7),
    (3, 5, 6, 7),
    (4, 5, 6, 7),
    (2, 4, 6, 7),
)


def dot(a, b, dims=((1,), (0,)), precision=None):
    return lax.dot_general(a, b, (dims, ((), ())), precision=precision, preferred_element_type=jnp.float32)


def kernel(
    hid_ref, og_ref, gain_ref, wg_ref, wu_ref, wd_ref, pm_ref, ph_ref, q_ref, out_ref,
    hid, og, nm, pm, ph, qb, rs, grid_in, wdb, wgb, wub, acc_a, acc_gu, rec_a, rec_gu, cols, cols_in, feat, feat_in,
    load_sem, w_sem, g_recv, own_send, core_send, relay_send, rs_send, rs_recv, q_send, q_recv,
    pa_send, pa_recv, px_send, px_recv, c_send, c_recv, f_send, f_recv,
):
    t = lax.axis_index("tp")
    s = lax.axis_index("sq")
    o = 1 - s
    rows, width = hid.shape
    bt = rows // NB
    hl = acc_a.shape[2]
    nc = hl // NC
    share = bt // 8

    def t_of(p):
        return jnp.where(p < 4, 2 * p, 15 - 2 * p)

    zz = t // 2
    pos = jnp.where(t % 2 == 0, zz, 7 - zz)
    right = t_of((pos + 1) % 8)
    left = t_of((pos + 7) % 8)
    place = (pos + 2 + 4 * s) % 8
    half = t // 4
    slot = t % 4

    def remote(src, dst, send, recv, dev):
        return pltpu.make_async_remote_copy(
            src_ref=src, dst_ref=dst, send_sem=send, recv_sem=recv, device_id=dev, device_id_type=MESH
        )

    loads = [
        pltpu.make_async_copy(hid_ref, hid, load_sem.at[0]),
        pltpu.make_async_copy(og_ref, og, load_sem.at[1]),
        pltpu.make_async_copy(pm_ref, pm, load_sem.at[2]),
        pltpu.make_async_copy(ph_ref, ph, load_sem.at[3]),
        pltpu.make_async_copy(q_ref, qb.at[s], load_sem.at[4]),
    ]
    for c in loads:
        c.start()

    steps = []
    for i in range(4):
        j = jnp.int32(0)
        for c in range(8):
            j = j + jnp.where(place == c, ARRIVALS[c][i], 0)
        dist = (j + 1) // 2
        odd = j % 2
        src_pos = (pos + 8 + dist * (1 - 2 * odd)) % 8
        src_slot = t_of(src_pos) % 4
        target = jnp.where(odd == 1, right, left)
        passes = [
            (j >= 1) & (dist < jnp.where(odd == 1, 4, 3)),
            (j >= 1) & (dist < jnp.where(odd == 1, 3, 4)),
        ]
        steps.append((src_slot, target, passes))

    def w_load(a, use):
        i, slot_at = USES[a][use][1], use % 2
        at = steps[i][0] * width
        at = pl.multiple_of(at, width)
        if a == 0:
            return [pltpu.make_async_copy(wd_ref.at[:, pl.ds(at, width)], wdb.at[slot_at], w_sem.at[0, slot_at])]
        return [
            pltpu.make_async_copy(wg_ref.at[pl.ds(at, width), :], wgb.at[slot_at], w_sem.at[1, slot_at]),
            pltpu.make_async_copy(wu_ref.at[pl.ds(at, width), :], wub.at[slot_at], w_sem.at[2, slot_at]),
        ]

    for a in range(2):
        for i in range(2):
            for c in w_load(a, i):
                c.start()

    barrier = pltpu.get_barrier_semaphore()
    for d in range(1, 8):
        pl.semaphore_signal(barrier, inc=1, device_id={"tp": (t + d) % 8}, device_id_type=MESH)
    for tt in (t, left, right):
        pl.semaphore_signal(barrier, inc=1, device_id={"tp": tt, "sq": o}, device_id_type=MESH)
    pl.semaphore_wait(barrier, 10)

    def own_copies(a, b):
        at = pl.ds(pl.multiple_of(b * bt, bt), bt)
        src = og_ref.at[at, :] if a == 0 else nm.at[at, :]
        dst = grid_in.at[a, b, slot, s]
        recv = g_recv.at[a, b, slot, s]
        away = [
            remote(src, dst, own_send.at[a, b, 0], recv, {"tp": right, "sq": half}),
            remote(src, dst, own_send.at[a, b, 1], recv, {"tp": left, "sq": half}),
        ]
        core = remote(src, dst, core_send.at[a, b], recv, {"sq": o})
        here = pltpu.make_async_copy(src, dst, recv)
        return away, core, here

    def own_start(a, b):
        away, core, here = own_copies(a, b)
        for c in away:
            c.start()

        @pl.when(half != s)
        def _():
            core.start()

        @pl.when(half == s)
        def _():
            here.start()

    def relays(a, b, i, k):
        src_slot, target, passes = steps[i]
        chunk = grid_in.at[a, b, src_slot, k]
        copy = remote(
            chunk, chunk, relay_send.at[a, b, i, k], g_recv.at[a, b, src_slot, k], {"tp": target}
        )
        return copy, passes[k]

    def arrive(a, b, i):
        for k in range(2):
            copy, passing = relays(a, b, i, k)
            copy.wait_recv()

            @pl.when(passing)
            def _():
                copy.start()

    own_start(0, 0)
    own_start(0, 1)
    q_copy = remote(q_ref, qb.at[s], q_send, q_recv, {"sq": o})
    q_copy.start()

    loads[0].wait()
    states = hid[...].astype(jnp.float32)
    sums = jnp.sum(states * states, axis=1, keepdims=True)
    rs[0] = jnp.transpose(jnp.broadcast_to(sums, (rows, 128)))[0:8]
    rs_copies = [
        remote(rs.at[0], rs.at[d], rs_send.at[d], rs_recv.at[d], {"tp": (t + d) % 8}) for d in range(1, 8)
    ]
    for c in rs_copies:
        c.start()
    loads[1].wait()
    loads[2].wait()
    c2 = dot(og[...], pm[2], ((1,), (1,)))
    for r, i in ORDER[:EARLY]:
        arrive(r // NB, r % NB, i)
    for c in rs_copies:
        c.wait_recv()
    total = rs[0]
    for d in range(1, 8):
        total = total + rs[d]
    factor = lax.rsqrt(total / D + EPS)
    factor = jnp.transpose(jnp.broadcast_to(factor[0:1], (128, rows)))[:, 0:1]
    nm[...] = (hid[...].astype(jnp.float32) * factor * gain_ref[...].astype(jnp.float32)).astype(jnp.bfloat16)
    own_start(1, 0)
    own_start(1, 1)
    c0 = dot(nm[...], pm[0], ((1,), (1,)))
    c1 = dot(nm[...], pm[1], ((1,), (1,)))
    for b in range(NB):
        part = slice(b * bt, (b + 1) * bt)
        cols[b, :, 0:128] = jnp.concatenate([c0[part], c1[part]], axis=1)
        cols[b, :, 128:256] = jnp.concatenate([c2[part], c2[part]], axis=1)
    loads[3].wait()

    def pa_copy(b):
        return remote(
            acc_a.at[b, pl.ds(pl.multiple_of(o * bt, bt), bt), :], rec_a.at[b], pa_send.at[b], pa_recv.at[b], {"sq": o}
        )

    def px_copy(b, n):
        lanes = pl.ds(pl.multiple_of(n * nc, nc), nc)
        return remote(
            acc_gu.at[b, :, pl.ds(pl.multiple_of(o * bt, bt), bt), lanes],
            rec_gu.at[b, :, :, lanes],
            px_send.at[b, n],
            px_recv.at[b, n],
            {"sq": o},
        )

    def c_copy(b, d):
        peer = (t + d) % 8
        return remote(
            cols.at[b, pl.ds(pl.multiple_of(peer * share, share), share), :],
            cols_in.at[b, d],
            c_send.at[b, d],
            c_recv.at[b, d],
            {"tp": peer},
        )

    def multiply(a, b, i):
        use = USES[a].index((a * NB + b, i))
        for c in w_load(a, use):
            c.wait()
        src_slot = steps[i][0]

        def part(n, carry):
            lanes = pl.ds(pl.multiple_of(n * nc, nc), nc)
            lhs = grid_in[a, b, src_slot].reshape(2 * bt, width)
            if a == 0:
                got = dot(lhs, wdb[use % 2, lanes, :], ((1,), (1,)))
                acc_a[b, :, lanes] = got if i == 0 else acc_a[b, :, lanes] + got
                return carry
            for m, buf in ((0, wgb), (1, wub)):
                got = dot(lhs, buf[use % 2, :, lanes])
                acc_gu[b, m, :, lanes] = got if i == 0 else acc_gu[b, m, :, lanes] + got
            if i == 3:
                px_copy(b, n).start()
            return carry

        lax.fori_loop(0, NC, part, 0)
        if use + 2 < len(USES[a]):
            for c in w_load(a, use + 2):
                c.start()
        if a == 0 and i == 3:
            pa_copy(b).start()

    def finish(b):
        pa_copy(b).wait_recv()
        mine = pl.ds(pl.multiple_of(s * bt, bt), bt)

        def hidden(n, carry):
            px_copy(b, n).wait_recv()
            lanes = pl.ds(pl.multiple_of(n * nc, nc), nc)
            gate = acc_gu[b, 0, mine, lanes] + rec_gu[b, 0, :, lanes]
            upward = acc_gu[b, 1, mine, lanes] + rec_gu[b, 1, :, lanes]
            grad_act = acc_a[b, mine, lanes] + rec_a[b, :, lanes]
            sig = jax.nn.sigmoid(gate)
            swish = gate * sig
            activation = (swish * upward).astype(jnp.bfloat16)
            grad_gate = (grad_act * upward * sig * (1.0 + gate * (1.0 - sig))).astype(jnp.bfloat16)
            grad_up = (grad_act * swish).astype(jnp.bfloat16)
            return (
                carry[0] + dot(grad_gate, ph[0, :, lanes], ((1,), (1,))),
                carry[1] + dot(grad_up, ph[1, :, lanes], ((1,), (1,))),
                carry[2] + dot(activation, ph[2, :, lanes], ((1,), (1,))),
            )

        zero = jnp.zeros((bt, R), jnp.float32)
        c3, c4, c5 = lax.fori_loop(0, NC, hidden, (zero, zero, zero))
        cols[b, :, 128:256] = jnp.concatenate([cols[b, :, 128:192], c3], axis=1)
        cols[b, :, 256:384] = jnp.concatenate([c4, c5], axis=1)
        for d in range(1, 8):
            c_copy(b, d).start()

    for at, (r, i) in enumerate(ORDER):
        if EARLY <= at + 1 < len(ORDER):
            ahead, step = ORDER[at + 1]
            arrive(ahead // NB, ahead % NB, step)
        multiply(r // NB, r % NB, i)
        if (r, i) == FINISH_AFTER:
            finish(0)
    finish(1)

    tokens = []
    for b in range(NB):
        whole = cols[b, pl.ds(pl.multiple_of(t * share, share), share), :]
        for d in range(1, 8):
            c_copy(b, d).wait_recv()
            whole = whole + cols_in[b, d]
        tokens.append(whole)
    tokens = jnp.concatenate(tokens, axis=0)
    row = lax.broadcasted_iota(jnp.int32, (R, R), 0)
    col = lax.broadcasted_iota(jnp.int32, (R, R), 1)
    order = jnp.where(row < R // 2, 2 * row, 2 * row - R + 1)
    pick = (col == order).astype(jnp.float32)
    for layer, (out_slot, in_slot) in enumerate(((3, 0), (4, 1), (2, 5))):
        outer = tokens[:, out_slot * R : (out_slot + 1) * R]
        inner = tokens[:, in_slot * R : (in_slot + 1) * R]
        pair = dot(outer, inner, ((0,), (0,)), HIGH)
        pair = dot(pick, pair, precision=HIGH)
        feat[layer * 32 : (layer + 1) * 32] = jnp.concatenate([pair[0:32], pair[32:64]], axis=1)
    f_copies = [remote(feat, feat_in.at[d], f_send.at[d], f_recv.at[d], {"tp": (t + d) % 8}) for d in range(1, 8)]
    for c in f_copies:
        c.start()
    loads[4].wait()
    q_copy.wait_recv()
    whole = feat[...]
    for d in range(1, 8):
        f_copies[d - 1].wait_recv()
        whole = whole + feat_in[d]
    acc = jnp.zeros((2, 16, 128), jnp.float32)
    for layer in range(3):
        for j in range(32):
            line = whole[layer * 32 + j : layer * 32 + j + 1]
            acc = acc + qb[:, layer, :, j * 128 : (j + 1) * 128].astype(jnp.float32) * line[None]
    out_ref[...] = dot(jnp.ones((1, 128), jnp.float32), acc.reshape(32, 128), ((1,), (1,)), HIGH)

    q_copy.wait_send()
    for c in rs_copies + f_copies:
        c.wait_send()

    def drain(b, carry):
        for a in range(2):
            away, core, _ = own_copies(a, b)
            for c in away:
                c.wait_send()

            @pl.when(half != s)
            def _():
                core.wait_send()

            for i in range(4):
                for k in range(2):
                    copy, passing = relays(a, b, i, k)

                    @pl.when(passing)
                    def _():
                        copy.wait_send()

        for d in range(1, 8):
            c_copy(b, d).wait_send()
        pa_copy(b).wait_send()
        for n in range(NC):
            px_copy(b, n).wait_send()
        return carry

    lax.fori_loop(0, NB, drain, 0)


def ring_device(hidden_states, out_grad, norm_gain, w_gate, w_up, w_down, proj_model, proj_hidden, queries):
    rows, width = hidden_states.shape
    hl = w_gate.shape[1]
    bt = rows // NB
    share = bt // 8
    bf, f32 = jnp.bfloat16, jnp.float32
    dma = pltpu.SemaphoreType.DMA
    anywhere = pl.BlockSpec(memory_space=pl.ANY)
    vmem = pl.BlockSpec(memory_space=pltpu.VMEM)
    return pl.pallas_call(
        kernel,
        out_shape=jax.ShapeDtypeStruct((1, 32), f32),
        in_specs=[anywhere, anywhere, vmem] + [anywhere] * 6,
        out_specs=vmem,
        scratch_shapes=[
            pltpu.VMEM((rows, width), bf),
            pltpu.VMEM((rows, width), bf),
            pltpu.VMEM((rows, width), bf),
            pltpu.VMEM((3, R, width), bf),
            pltpu.VMEM((3, R, hl), bf),
            pltpu.VMEM((2,) + queries.shape, bf),
            pltpu.VMEM((8, 8, rows), f32),
            pltpu.VMEM((2, NB, 4, 2, bt, width), bf),
            pltpu.VMEM((2, hl, width), bf),
            pltpu.VMEM((2, width, hl), bf),
            pltpu.VMEM((2, width, hl), bf),
            pltpu.VMEM((NB, 2 * bt, hl), f32),
            pltpu.VMEM((NB, 2, 2 * bt, hl), f32),
            pltpu.VMEM((NB, bt, hl), f32),
            pltpu.VMEM((NB, 2, bt, hl), f32),
            pltpu.VMEM((NB, bt, 6 * R), f32),
            pltpu.VMEM((NB, 8, share, 6 * R), f32),
            pltpu.VMEM((96, 128), f32),
            pltpu.VMEM((8, 96, 128), f32),
            dma((5,)),
            dma((3, 2)),
            dma((2, NB, 4, 2)),
            dma((2, NB, 2)),
            dma((2, NB)),
            dma((2, NB, 4, 2)),
            dma((8,)),
            dma((8,)),
            dma,
            dma,
            dma((NB,)),
            dma((NB,)),
            dma((NB, NC)),
            dma((NB, NC)),
            dma((NB, 8)),
            dma((NB, 8)),
            dma((8,)),
            dma((8,)),
        ],
        compiler_params=pltpu.CompilerParams(
            collective_id=0, has_side_effects=True, vmem_limit_bytes=60 * 1024 * 1024
        ),
        cost_estimate=pl.CostEstimate(flops=26 * 10**9, bytes_accessed=10**8, transcendentals=10**6),
    )(
        hidden_states,
        out_grad,
        norm_gain.reshape(1, width),
        w_gate,
        w_up,
        w_down,
        jnp.swapaxes(proj_model, 1, 2),
        jnp.swapaxes(proj_hidden, 1, 2),
        queries,
    )


def layer_features(columns, member):
    slot_pairs = ((3, 0), (4, 1), (2, 5))
    result = []
    for out_slot, in_slot in slot_pairs:
        outer = columns[:, out_slot * R : (out_slot + 1) * R]
        inner = columns[:, in_slot * R : (in_slot + 1) * R]
        block = jnp.einsum("te,to,ti->eoi", member, outer, inner, precision=HIGH)
        result.append(block.reshape(member.shape[1], R * R))
    return jnp.stack(result, axis=1)


def membership(row_count, seq_count):
    token_seq = jnp.arange(row_count, dtype=jnp.int32) // SEQ_LEN
    return (token_seq[:, None] == jnp.arange(seq_count, dtype=jnp.int32)[None, :]).astype(jnp.float32)


def wide_device(hidden_states, out_grad, norm_gain, w_gate, w_up, w_down, proj_model, proj_hidden, queries):
    gate_full, up_full, down_full = (
        lax.all_gather(w_gate, "sq", axis=0, tiled=True),
        lax.all_gather(w_up, "sq", axis=0, tiled=True),
        lax.all_gather(w_down, "sq", axis=1, tiled=True),
    )
    row_count = hidden_states.shape[0]
    seq_count = row_count // SEQ_LEN
    states = hidden_states.astype(jnp.float32)
    row_total = lax.psum(jnp.sum(states * states, axis=1), "tp")
    factor = lax.rsqrt(row_total / D + EPS)
    normed = (states * factor[:, None] * norm_gain.astype(jnp.float32)).astype(jnp.bfloat16)
    shard_piece = lax.all_gather(normed, "tp", axis=1, tiled=True)
    gate = jnp.dot(shard_piece, gate_full, preferred_element_type=jnp.float32)
    upward = jnp.dot(shard_piece, up_full, preferred_element_type=jnp.float32)
    grad_act = lax.dot_general(
        lax.all_gather(out_grad, "tp", axis=1, tiled=True),
        down_full,
        (((1,), (1,)), ((), ())),
        preferred_element_type=jnp.float32,
    )
    sigmoid_gate = jax.nn.sigmoid(gate)
    swish = gate * sigmoid_gate
    activation = (swish * upward).astype(jnp.bfloat16)
    grad_gate = (grad_act * upward * sigmoid_gate * (1.0 + gate * (1.0 - sigmoid_gate))).astype(jnp.bfloat16)
    grad_up = (grad_act * swish).astype(jnp.bfloat16)
    sources = (normed, normed, out_grad, grad_gate, grad_up, activation)
    pieces = []
    for i, source in enumerate(sources):
        table = proj_model[i] if i < 3 else proj_hidden[i - 3]
        pieces.append(jnp.dot(source, table, preferred_element_type=jnp.float32))
    columns = lax.psum(jnp.concatenate(pieces, axis=1), "tp")
    features = layer_features(columns, membership(row_count, seq_count))
    paired = lax.all_gather(queries, "sq", axis=1, tiled=True)
    return jnp.einsum("elk,lqk->eq", features, paired.astype(jnp.float32), precision=HIGH)


def solution(mesh):
    placed = (
        P(("groups", "sq"), "tp"),
        P(("groups", "sq"), "tp"),
        P("tp"),
        P("sq", "tp"),
        P("sq", "tp"),
        P("tp", "sq"),
        P(None, "tp", None),
        P(None, "tp", None),
        P(None, ("tp", "sq"), None),
    )
    body = ring_device if mesh.shape["tp"] == 8 else wide_device
    return jax.shard_map(
        body, mesh=mesh, in_specs=placed, out_specs=P(("groups", "sq"), "tp"), check_vma=False
    )
```

```python
import functools

import jax
import jax.numpy as jnp
from jax import lax
from jax.experimental import pallas as pl
from jax.experimental.pallas import tpu as pltpu
from jax.sharding import PartitionSpec as P

D = 8192
R = 64
SEQ_LEN = 256
EPS = 1e-05
NB = 2
NC = 4
MESH = pl.DeviceIdType.MESH
HIGH = lax.Precision.HIGHEST
ORDER = tuple(sorted(((r, i) for r in range(2 * NB) for i in range(4)), key=lambda e: 7 * e[0] + 6 * e[1]))
EARLY = 2
FINISH_AFTER = ORDER[ORDER.index((2, 3)) + 1]
USES = tuple(tuple(e for e in ORDER if e[0] // NB == a) for a in range(2))
ARRIVALS = (
    (0, 2, 4, 6),
    (0, 1, 2, 4),
    (0, 1, 2, 3),
    (0, 1, 3, 5),
    (1, 3, 5, 7),
    (3, 5, 6, 7),
    (4, 5, 6, 7),
    (2, 4, 6, 7),
)


def dot(a, b, dims=((1,), (0,)), precision=None):
    return lax.dot_general(a, b, (dims, ((), ())), precision=precision, preferred_element_type=jnp.float32)


def kernel(
    hid_ref, og_ref, gain_ref, wg_ref, wu_ref, wd_ref, pm_ref, ph_ref, q_ref, out_ref,
    hid, og, nm, pm, ph, qb, rs, grid_in, wdb, wgb, wub, acc_a, acc_gu, rec_a, rec_gu, cols, cols_in, feat, feat_in,
    load_sem, w_sem, g_recv, own_send, core_send, relay_send, rs_send, rs_recv, q_send, q_recv,
    pa_send, pa_recv, px_send, px_recv, c_send, c_recv, f_send, f_recv,
):
    t = lax.axis_index("tp")
    s = lax.axis_index("sq")
    o = 1 - s
    rows, width = hid.shape
    bt = rows // NB
    hl = acc_a.shape[2]
    nc = hl // NC
    share = bt // 8

    def t_of(p):
        return jnp.where(p < 4, 2 * p, 15 - 2 * p)

    zz = t // 2
    pos = jnp.where(t % 2 == 0, zz, 7 - zz)
    right = t_of((pos + 1) % 8)
    left = t_of((pos + 7) % 8)
    place = (pos + 2 + 4 * s) % 8
    half = t // 4
    slot = t % 4

    def remote(src, dst, send, recv, dev):
        return pltpu.make_async_remote_copy(
            src_ref=src, dst_ref=dst, send_sem=send, recv_sem=recv, device_id=dev, device_id_type=MESH
        )

    loads = [
        pltpu.make_async_copy(hid_ref, hid, load_sem.at[0]),
        pltpu.make_async_copy(og_ref, og, load_sem.at[1]),
        pltpu.make_async_copy(pm_ref, pm, load_sem.at[2]),
        pltpu.make_async_copy(ph_ref, ph, load_sem.at[3]),
        pltpu.make_async_copy(q_ref, qb.at[s], load_sem.at[4]),
    ]
    for c in loads:
        c.start()

    steps = []
    for i in range(4):
        j = jnp.int32(0)
        for c in range(8):
            j = j + jnp.where(place == c, ARRIVALS[c][i], 0)
        dist = (j + 1) // 2
        odd = j % 2
        src_pos = (pos + 8 + dist * (1 - 2 * odd)) % 8
        src_slot = t_of(src_pos) % 4
        target = jnp.where(odd == 1, right, left)
        passes = [
            (j >= 1) & (dist < jnp.where(odd == 1, 4, 3)),
            (j >= 1) & (dist < jnp.where(odd == 1, 3, 4)),
        ]
        steps.append((src_slot, target, passes))

    def w_load(a, use):
        i, slot_at = USES[a][use][1], use % 2
        at = steps[i][0] * width
        at = pl.multiple_of(at, width)
        if a == 0:
            return [pltpu.make_async_copy(wd_ref.at[:, pl.ds(at, width)], wdb.at[slot_at], w_sem.at[0, slot_at])]
        return [
            pltpu.make_async_copy(wg_ref.at[pl.ds(at, width), :], wgb.at[slot_at], w_sem.at[1, slot_at]),
            pltpu.make_async_copy(wu_ref.at[pl.ds(at, width), :], wub.at[slot_at], w_sem.at[2, slot_at]),
        ]

    for a in range(2):
        for i in range(2):
            for c in w_load(a, i):
                c.start()

    barrier = pltpu.get_barrier_semaphore()
    for d in range(1, 8):
        pl.semaphore_signal(barrier, inc=1, device_id={"tp": (t + d) % 8}, device_id_type=MESH)
    for tt in (t, left, right):
        pl.semaphore_signal(barrier, inc=1, device_id={"tp": tt, "sq": o}, device_id_type=MESH)
    pl.semaphore_wait(barrier, 10)

    def own_copies(a, b):
        at = pl.ds(pl.multiple_of(b * bt, bt), bt)
        src = og_ref.at[at, :] if a == 0 else nm.at[at, :]
        dst = grid_in.at[a, b, slot, s]
        recv = g_recv.at[a, b, slot, s]
        away = [
            remote(src, dst, own_send.at[a, b, 0], recv, {"tp": right, "sq": half}),
            remote(src, dst, own_send.at[a, b, 1], recv, {"tp": left, "sq": half}),
        ]
        core = remote(src, dst, core_send.at[a, b], recv, {"sq": o})
        here = pltpu.make_async_copy(src, dst, recv)
        return away, core, here

    def own_start(a, b):
        away, core, here = own_copies(a, b)
        for c in away:
            c.start()

        @pl.when(half != s)
        def _():
            core.start()

        @pl.when(half == s)
        def _():
            here.start()

    def relays(a, b, i, k):
        src_slot, target, passes = steps[i]
        chunk = grid_in.at[a, b, src_slot, k]
        copy = remote(
            chunk, chunk, relay_send.at[a, b, i, k], g_recv.at[a, b, src_slot, k], {"tp": target}
        )
        return copy, passes[k]

    def arrive(a, b, i):
        for k in range(2):
            copy, passing = relays(a, b, i, k)
            copy.wait_recv()

            @pl.when(passing)
            def _():
                copy.start()

    own_start(0, 0)
    own_start(0, 1)
    q_copy = remote(q_ref, qb.at[s], q_send, q_recv, {"sq": o})
    q_copy.start()

    loads[0].wait()
    states = hid[...].astype(jnp.float32)
    sums = jnp.sum(states * states, axis=1, keepdims=True)
    rs[0] = jnp.transpose(jnp.broadcast_to(sums, (rows, 128)))[0:8]
    rs_copies = [
        remote(rs.at[0], rs.at[d], rs_send.at[d], rs_recv.at[d], {"tp": (t + d) % 8}) for d in range(1, 8)
    ]
    for c in rs_copies:
        c.start()
    loads[1].wait()
    loads[2].wait()
    c2 = dot(og[...], pm[2], ((1,), (1,)))
    for r, i in ORDER[:EARLY]:
        arrive(r // NB, r % NB, i)
    for c in rs_copies:
        c.wait_recv()
    total = rs[0]
    for d in range(1, 8):
        total = total + rs[d]
    factor = lax.rsqrt(total / D + EPS)
    factor = jnp.transpose(jnp.broadcast_to(factor[0:1], (128, rows)))[:, 0:1]
    nm[...] = (hid[...].astype(jnp.float32) * factor * gain_ref[...].astype(jnp.float32)).astype(jnp.bfloat16)
    own_start(1, 0)
    own_start(1, 1)
    c0 = dot(nm[...], pm[0], ((1,), (1,)))
    c1 = dot(nm[...], pm[1], ((1,), (1,)))
    for b in range(NB):
        part = slice(b * bt, (b + 1) * bt)
        cols[b, :, 0:128] = jnp.concatenate([c0[part], c1[part]], axis=1)
        cols[b, :, 128:256] = jnp.concatenate([c2[part], c2[part]], axis=1)
    loads[3].wait()

    def pa_copy(b):
        return remote(
            acc_a.at[b, pl.ds(pl.multiple_of(o * bt, bt), bt), :], rec_a.at[b], pa_send.at[b], pa_recv.at[b], {"sq": o}
        )

    def px_copy(b, n):
        lanes = pl.ds(pl.multiple_of(n * nc, nc), nc)
        return remote(
            acc_gu.at[b, :, pl.ds(pl.multiple_of(o * bt, bt), bt), lanes],
            rec_gu.at[b, :, :, lanes],
            px_send.at[b, n],
            px_recv.at[b, n],
            {"sq": o},
        )

    def c_copy(b, d):
        peer = (t + d) % 8
        return remote(
            cols.at[b, pl.ds(pl.multiple_of(peer * share, share), share), :],
            cols_in.at[b, d],
            c_send.at[b, d],
            c_recv.at[b, d],
            {"tp": peer},
        )

    def multiply(a, b, i):
        use = USES[a].index((a * NB + b, i))
        for c in w_load(a, use):
            c.wait()
        src_slot = steps[i][0]

        def part(n, carry):
            lanes = pl.ds(pl.multiple_of(n * nc, nc), nc)
            lhs = grid_in[a, b, src_slot].reshape(2 * bt, width)
            if a == 0:
                got = dot(lhs, wdb[use % 2, lanes, :], ((1,), (1,)))
                acc_a[b, :, lanes] = got if i == 0 else acc_a[b, :, lanes] + got
                return carry
            for m, buf in ((0, wgb), (1, wub)):
                got = dot(lhs, buf[use % 2, :, lanes])
                acc_gu[b, m, :, lanes] = got if i == 0 else acc_gu[b, m, :, lanes] + got
            if i == 3:
                px_copy(b, n).start()
            return carry

        lax.fori_loop(0, NC, part, 0)
        if use + 2 < len(USES[a]):
            for c in w_load(a, use + 2):
                c.start()
        if a == 0 and i == 3:
            pa_copy(b).start()

    def finish(b):
        pa_copy(b).wait_recv()
        mine = pl.ds(pl.multiple_of(s * bt, bt), bt)

        def hidden(n, carry):
            px_copy(b, n).wait_recv()
            lanes = pl.ds(pl.multiple_of(n * nc, nc), nc)
            gate = acc_gu[b, 0, mine, lanes] + rec_gu[b, 0, :, lanes]
            upward = acc_gu[b, 1, mine, lanes] + rec_gu[b, 1, :, lanes]
            grad_act = acc_a[b, mine, lanes] + rec_a[b, :, lanes]
            sig = jax.nn.sigmoid(gate)
            swish = gate * sig
            activation = (swish * upward).astype(jnp.bfloat16)
            grad_gate = (grad_act * upward * sig * (1.0 + gate * (1.0 - sig))).astype(jnp.bfloat16)
            grad_up = (grad_act * swish).astype(jnp.bfloat16)
            return (
                carry[0] + dot(grad_gate, ph[0, :, lanes], ((1,), (1,))),
                carry[1] + dot(grad_up, ph[1, :, lanes], ((1,), (1,))),
                carry[2] + dot(activation, ph[2, :, lanes], ((1,), (1,))),
            )

        zero = jnp.zeros((bt, R), jnp.float32)
        c3, c4, c5 = lax.fori_loop(0, NC, hidden, (zero, zero, zero))
        cols[b, :, 128:256] = jnp.concatenate([cols[b, :, 128:192], c3], axis=1)
        cols[b, :, 256:384] = jnp.concatenate([c4, c5], axis=1)
        for d in range(1, 8):
            c_copy(b, d).start()

    for at, (r, i) in enumerate(ORDER):
        if EARLY <= at + 1 < len(ORDER) - 1:
            ahead, step = ORDER[at + 1]
            arrive(ahead // NB, ahead % NB, step)
        if at == len(ORDER) - 2:

            @pl.when(place < 4)
            def _():
                arrive(1, NB - 1, 3)

        if at == len(ORDER) - 1:

            @pl.when(place >= 4)
            def _():
                arrive(1, NB - 1, 3)

        multiply(r // NB, r % NB, i)
        if (r, i) == FINISH_AFTER:
            finish(0)
    finish(1)

    tokens = []
    for b in range(NB):
        whole = cols[b, pl.ds(pl.multiple_of(t * share, share), share), :]
        for d in range(1, 8):
            c_copy(b, d).wait_recv()
            whole = whole + cols_in[b, d]
        tokens.append(whole)
    tokens = jnp.concatenate(tokens, axis=0)
    row = lax.broadcasted_iota(jnp.int32, (R, R), 0)
    col = lax.broadcasted_iota(jnp.int32, (R, R), 1)
    order = jnp.where(row < R // 2, 2 * row, 2 * row - R + 1)
    pick = (col == order).astype(jnp.float32)
    for layer, (out_slot, in_slot) in enumerate(((3, 0), (4, 1), (2, 5))):
        outer = tokens[:, out_slot * R : (out_slot + 1) * R]
        inner = tokens[:, in_slot * R : (in_slot + 1) * R]
        pair = dot(outer, inner, ((0,), (0,)), HIGH)
        pair = dot(pick, pair, precision=HIGH)
        feat[layer * 32 : (layer + 1) * 32] = jnp.concatenate([pair[0:32], pair[32:64]], axis=1)
    f_copies = [remote(feat, feat_in.at[d], f_send.at[d], f_recv.at[d], {"tp": (t + d) % 8}) for d in range(1, 8)]
    for c in f_copies:
        c.start()
    loads[4].wait()
    q_copy.wait_recv()
    whole = feat[...]
    for d in range(1, 8):
        f_copies[d - 1].wait_recv()
        whole = whole + feat_in[d]
    acc = jnp.zeros((2, 16, 128), jnp.float32)
    for layer in range(3):
        for j in range(32):
            line = whole[layer * 32 + j : layer * 32 + j + 1]
            acc = acc + qb[:, layer, :, j * 128 : (j + 1) * 128].astype(jnp.float32) * line[None]
    out_ref[...] = dot(jnp.ones((1, 128), jnp.float32), acc.reshape(32, 128), ((1,), (1,)), HIGH)

    q_copy.wait_send()
    for c in rs_copies + f_copies:
        c.wait_send()

    def drain(b, carry):
        for a in range(2):
            away, core, _ = own_copies(a, b)
            for c in away:
                c.wait_send()

            @pl.when(half != s)
            def _():
                core.wait_send()

            for i in range(4):
                for k in range(2):
                    copy, passing = relays(a, b, i, k)

                    @pl.when(passing)
                    def _():
                        copy.wait_send()

        for d in range(1, 8):
            c_copy(b, d).wait_send()
        pa_copy(b).wait_send()
        for n in range(NC):
            px_copy(b, n).wait_send()
        return carry

    lax.fori_loop(0, NB, drain, 0)


def ring_device(hidden_states, out_grad, norm_gain, w_gate, w_up, w_down, proj_model, proj_hidden, queries):
    rows, width = hidden_states.shape
    hl = w_gate.shape[1]
    bt = rows // NB
    share = bt // 8
    bf, f32 = jnp.bfloat16, jnp.float32
    dma = pltpu.SemaphoreType.DMA
    anywhere = pl.BlockSpec(memory_space=pl.ANY)
    vmem = pl.BlockSpec(memory_space=pltpu.VMEM)
    return pl.pallas_call(
        kernel,
        out_shape=jax.ShapeDtypeStruct((1, 32), f32),
        in_specs=[anywhere, anywhere, vmem] + [anywhere] * 6,
        out_specs=vmem,
        scratch_shapes=[
            pltpu.VMEM((rows, width), bf),
            pltpu.VMEM((rows, width), bf),
            pltpu.VMEM((rows, width), bf),
            pltpu.VMEM((3, R, width), bf),
            pltpu.VMEM((3, R, hl), bf),
            pltpu.VMEM((2,) + queries.shape, bf),
            pltpu.VMEM((8, 8, rows), f32),
            pltpu.VMEM((2, NB, 4, 2, bt, width), bf),
            pltpu.VMEM((2, hl, width), bf),
            pltpu.VMEM((2, width, hl), bf),
            pltpu.VMEM((2, width, hl), bf),
            pltpu.VMEM((NB, 2 * bt, hl), f32),
            pltpu.VMEM((NB, 2, 2 * bt, hl), f32),
            pltpu.VMEM((NB, bt, hl), f32),
            pltpu.VMEM((NB, 2, bt, hl), f32),
            pltpu.VMEM((NB, bt, 6 * R), f32),
            pltpu.VMEM((NB, 8, share, 6 * R), f32),
            pltpu.VMEM((96, 128), f32),
            pltpu.VMEM((8, 96, 128), f32),
            dma((5,)),
            dma((3, 2)),
            dma((2, NB, 4, 2)),
            dma((2, NB, 2)),
            dma((2, NB)),
            dma((2, NB, 4, 2)),
            dma((8,)),
            dma((8,)),
            dma,
            dma,
            dma((NB,)),
            dma((NB,)),
            dma((NB, NC)),
            dma((NB, NC)),
            dma((NB, 8)),
            dma((NB, 8)),
            dma((8,)),
            dma((8,)),
        ],
        compiler_params=pltpu.CompilerParams(
            collective_id=0, has_side_effects=True, vmem_limit_bytes=60 * 1024 * 1024
        ),
        cost_estimate=pl.CostEstimate(flops=26 * 10**9, bytes_accessed=10**8, transcendentals=10**6),
    )(
        hidden_states,
        out_grad,
        norm_gain.reshape(1, width),
        w_gate,
        w_up,
        w_down,
        jnp.swapaxes(proj_model, 1, 2),
        jnp.swapaxes(proj_hidden, 1, 2),
        queries,
    )


def layer_features(columns, member):
    slot_pairs = ((3, 0), (4, 1), (2, 5))
    result = []
    for out_slot, in_slot in slot_pairs:
        outer = columns[:, out_slot * R : (out_slot + 1) * R]
        inner = columns[:, in_slot * R : (in_slot + 1) * R]
        block = jnp.einsum("te,to,ti->eoi", member, outer, inner, precision=HIGH)
        result.append(block.reshape(member.shape[1], R * R))
    return jnp.stack(result, axis=1)


def membership(row_count, seq_count):
    token_seq = jnp.arange(row_count, dtype=jnp.int32) // SEQ_LEN
    return (token_seq[:, None] == jnp.arange(seq_count, dtype=jnp.int32)[None, :]).astype(jnp.float32)


def wide_device(hidden_states, out_grad, norm_gain, w_gate, w_up, w_down, proj_model, proj_hidden, queries):
    gate_full, up_full, down_full = (
        lax.all_gather(w_gate, "sq", axis=0, tiled=True),
        lax.all_gather(w_up, "sq", axis=0, tiled=True),
        lax.all_gather(w_down, "sq", axis=1, tiled=True),
    )
    row_count = hidden_states.shape[0]
    seq_count = row_count // SEQ_LEN
    states = hidden_states.astype(jnp.float32)
    row_total = lax.psum(jnp.sum(states * states, axis=1), "tp")
    factor = lax.rsqrt(row_total / D + EPS)
    normed = (states * factor[:, None] * norm_gain.astype(jnp.float32)).astype(jnp.bfloat16)
    shard_piece = lax.all_gather(normed, "tp", axis=1, tiled=True)
    gate = jnp.dot(shard_piece, gate_full, preferred_element_type=jnp.float32)
    upward = jnp.dot(shard_piece, up_full, preferred_element_type=jnp.float32)
    grad_act = lax.dot_general(
        lax.all_gather(out_grad, "tp", axis=1, tiled=True),
        down_full,
        (((1,), (1,)), ((), ())),
        preferred_element_type=jnp.float32,
    )
    sigmoid_gate = jax.nn.sigmoid(gate)
    swish = gate * sigmoid_gate
    activation = (swish * upward).astype(jnp.bfloat16)
    grad_gate = (grad_act * upward * sigmoid_gate * (1.0 + gate * (1.0 - sigmoid_gate))).astype(jnp.bfloat16)
    grad_up = (grad_act * swish).astype(jnp.bfloat16)
    sources = (normed, normed, out_grad, grad_gate, grad_up, activation)
    pieces = []
    for i, source in enumerate(sources):
        table = proj_model[i] if i < 3 else proj_hidden[i - 3]
        pieces.append(jnp.dot(source, table, preferred_element_type=jnp.float32))
    columns = lax.psum(jnp.concatenate(pieces, axis=1), "tp")
    features = layer_features(columns, membership(row_count, seq_count))
    paired = lax.all_gather(queries, "sq", axis=1, tiled=True)
    return jnp.einsum("elk,lqk->eq", features, paired.astype(jnp.float32), precision=HIGH)


def solution(mesh):
    placed = (
        P(("groups", "sq"), "tp"),
        P(("groups", "sq"), "tp"),
        P("tp"),
        P("sq", "tp"),
        P("sq", "tp"),
        P("tp", "sq"),
        P(None, "tp", None),
        P(None, "tp", None),
        P(None, ("tp", "sq"), None),
    )
    body = ring_device if mesh.shape["tp"] == 8 else wide_device
    return jax.shard_map(
        body, mesh=mesh, in_specs=placed, out_specs=P(("groups", "sq"), "tp"), check_vma=False
    )
```
